32 devices in a mesh: ctx: 16 (over z, x, core), ch: 2 (over y).
Axes of the slice: x: 2, y: 2, z: 4, core: 2. Of those that a mesh axis runs over, the one named last changes fastest.
Arguments:
- projections: bfloat16 [3, 4096, 8192], P(None, ('ctx', 'ch')), may hold values from -3 to 3
- attention_order: int32 [4096], replicated, may hold values from 0 to 4095, as said below
- doc_lengths: int32 [4], replicated, may hold values from 1 to 2048, 4096 in all
- short_filter: float32 [3, 3, 8192], P(None, None, 'ch'), may hold values from -3.5 to 3.5
- decay_rate: float32 [512, 16], P('ch'), may hold values from 2.4414063e-05 to 0.03
- residue: float32 [512, 16], P('ch'), may hold values from -1.5 to 1.5
- skip_gain: float32 [8192], P('ch'), may hold values from -2.5 to 2.5
Outputs:
- mixed_rows: bfloat16 [4096, 8192], P(('ctx', 'ch'))
The draws below stay inside these ranges and needn't reach their ends.
Inputs may be any that keep to these rules, and one draw needn't show every extreme that they name: `attention_order`: A permutation of the 4096 positions. For every group a of 256 rows (rows a * 256 to (a + 1) * 256 - 1) and every context block j, the rows a * 256 + j * 16 to a * 256 + (j + 1) * 16 - 1 hold positions of block j, that is j * 256 to (j + 1) * 256 - 1, in any order. `doc_lengths`: the documents lie one after another in the slab; the lengths sum to 4096.
All inputs are finite; a program needn't handle non-finite values.
Results may differ from the reference program's by a relative error of at most 0.0049.
Values may be sent and summed in bfloat16 or wider, within the bound.
A program may use at most 128 MiB of HBM per device.

```python
import math
import jax
import jax.numpy as jnp
import numpy as np
from jax import lax

D = 8192
MODES = 16
FILTER_CHANNELS = 16
DOCS = 4
TOK_DEV = 256
TOKENS = 4096
FILTERS = 512


def draw_attention_order(key, part):
    block_total = TOKENS // TOK_DEV
    slot_rows = TOK_DEV // block_total
    subkeys = jax.random.split(key, block_total)
    shuffled = jax.vmap(lambda subkey: jax.random.permutation(subkey, TOK_DEV))(subkeys).astype(jnp.int32)
    positions = shuffled + (jnp.arange(block_total, dtype=jnp.int32) * TOK_DEV)[:, None]
    arranged = jnp.transpose(positions.reshape(block_total, block_total, slot_rows), (1, 0, 2))
    return arranged.reshape(TOKENS).astype(jnp.int32)


def levels(rng, dims, cuts, least, high):
    def one(axis_at, shards_of):
        draws = jax.random.uniform(jax.random.fold_in(jax.random.fold_in(rng, 6), axis_at), (shards_of,), jnp.float32, least / len(cuts), high / len(cuts))
        return jnp.repeat(jnp.exp(draws), dims[axis_at] // shards_of).reshape((-1,) + (1,) * (len(dims) - axis_at - 1))

    factor_of = one(*cuts[0])
    for cut in cuts[1:]:
        factor_of = factor_of * one(*cut)
    return factor_of


def split_up(amount, total, limit, skew):
    loads = [(1 << 20) // math.isqrt(grade ** skew) + 1 for grade in range(2, amount + 1)]
    surplus, holding = total - limit - (amount - 1), [1] * (amount - 1)
    while surplus > 0:
        candidates = [i for i in range(amount - 1) if holding[i] < limit]
        pool, budget = sum([loads[i] for i in candidates]), surplus
        for i in candidates:
            more = min(limit - holding[i], max(1, budget * loads[i] // pool), surplus)
            holding[i] = holding[i] + more
            surplus = surplus - more
    return np.array([limit] + holding)


def uneven_parts(own_key, amount, total, bound, skew):
    if amount == 2:
        one = jax.random.randint(own_key, (), max(1, total - bound), min(bound, total - 1) + 1)
        return jnp.stack([one, total - one])
    tallies = jnp.asarray(split_up(amount, total, bound, skew), jnp.int32)
    couples = (amount - 1) // 2
    giver, sink = tallies[1:1 + 2 * couples:2], tallies[2:2 + 2 * couples:2]
    margin = jnp.minimum(giver - 1, bound - sink)
    moved = jax.random.randint(jax.random.fold_in(own_key, 1), (couples,), 0, 1 << 20) % (margin + 1)
    tallies = tallies.at[1:1 + 2 * couples:2].set(giver - moved).at[2:2 + 2 * couples:2].set(sink + moved)
    return tallies[jax.random.permutation(jax.random.fold_in(own_key, 2), amount)]


def scatter_about(stream_key, shape, width, limit, pieces=(), held_as=jnp.bfloat16):
    factor_of = levels(stream_key, shape, pieces, -0.22, 0.18) if pieces else 1.0
    array = jax.random.normal(stream_key, shape, jnp.float32) * width * factor_of
    return jnp.minimum(jnp.maximum(array, -limit), limit).astype(held_as)


def setup_inputs(seed: int = 0) -> dict:
    seeds = jax.random.split(jax.random.key(seed), 8)
    projections = scatter_about(seeds[0], (3, TOKENS, D), 1.0, 3.0, ((1, 32),))
    attention_order = draw_attention_order(jax.random.fold_in(seeds[7], 71), 0)
    doc_lengths = uneven_parts(seeds[2], DOCS, TOKENS, TOKENS // 2, 2).astype(jnp.int32)
    short_filter = scatter_about(seeds[3], (3, 3, D), 3 ** -0.5, 3.5, ((2, 2),), jnp.float32)
    decay_rate = jnp.clip(jnp.exp(math.log(0.03) - 7.1137933 * jax.random.uniform(seeds[4], (FILTERS, MODES), jnp.float32) ** levels(seeds[4], (FILTERS, MODES), ((0, 2),), -0.2, 0.2)), 2.441406286379788e-05, 0.03)
    residue = scatter_about(seeds[5], (FILTERS, MODES), 0.25, 1.5, ((0, 2),), jnp.float32)
    skip_gain = scatter_about(seeds[6], (D,), 1.0, 2.5, ((0, 2),), jnp.float32)
    return dict(projections=projections, attention_order=attention_order, doc_lengths=doc_lengths, short_filter=short_filter, decay_rate=decay_rate, residue=residue, skip_gain=skip_gain)


def reference(projections, attention_order, doc_lengths, short_filter, decay_rate, residue, skip_gain):
    positions = jnp.arange(TOKENS, dtype=jnp.int32)
    inverse = jnp.zeros((TOKENS,), jnp.int32).at[attention_order].set(positions)
    bounds = jnp.cumsum(doc_lengths).astype(jnp.int32)
    document = lax.optimization_barrier(jnp.sum((positions[:, None] >= bounds[None, :]).astype(jnp.int32), axis=1)).astype(jnp.int32)
    coefficient = residue * jnp.sqrt(1.0 - jnp.exp(-2.0 * decay_rate))
    decay_wide = jnp.repeat(jnp.exp(-decay_rate).T, FILTER_CHANNELS, axis=1)
    coeff_wide = jnp.repeat(coefficient.T, FILTER_CHANNELS, axis=1)

    def advance(carry, inputs):
        state, back_one, back_two, doc_one, doc_two = carry
        source, doc_now = inputs
        current_row = lax.dynamic_slice_in_dim(projections, source.astype(jnp.int32), 1, 1)[:, 0, :].astype(jnp.float32)
        keep_one = (doc_one == doc_now).astype(jnp.float32)
        keep_two = (doc_two == doc_now).astype(jnp.float32)
        featured = short_filter[:, 0, :] * current_row + short_filter[:, 1, :] * back_one * keep_one + short_filter[:, 2, :] * back_two * keep_two
        gated = (featured[1] * featured[2]).astype(jnp.bfloat16)
        gated_wide = lax.optimization_barrier(gated).astype(jnp.float32)
        state = decay_wide * state * keep_one + gated_wide[None, :]
        mixed = featured[0] * (lax.optimization_barrier(jnp.sum(coeff_wide * state, axis=0)) + skip_gain * gated_wide)
        return ((state, current_row, back_one, doc_now, doc_one), mixed.astype(jnp.bfloat16))
    initial = (jnp.zeros((MODES, D), jnp.float32), jnp.zeros((3, D), jnp.float32), jnp.zeros((3, D), jnp.float32), jnp.int32(-1), jnp.int32(-1))
    final_carry, mixed = lax.scan(advance, initial, (inverse, document))
    return jnp.take(mixed, attention_order, axis=0)
```

```python
import functools

import jax
import jax.numpy as jnp
from jax import lax
from jax.experimental import pallas as pl
from jax.experimental.pallas import tpu as pltpu
from jax.sharding import PartitionSpec as P

LANES = 128

highest = lax.Precision.HIGHEST


def from_behind(value, axis, steps):
    count = lax.axis_size(axis)
    first, last = (max(0, -steps), min(count, count - steps))
    return lax.ppermute(value, axis, [(source, source + steps) for source in range(first, last)])


def entering(value, axis, combine, identity):
    devices, here = (lax.axis_size(axis), lax.axis_index(axis))
    everything = jax.tree.map(lambda part: lax.all_gather(part, axis), value)
    start = jax.tree.map(
        lambda part, zero: jnp.broadcast_to(jnp.asarray(zero, part.dtype), part.shape),
        value,
        identity,
    )

    def turn(k, before):
        reached = k < here
        new = combine(before, jax.tree.map(lambda part: part[k], everything))
        return jax.tree.map(lambda a, b: jnp.where(reached, a, b), new, before)

    return lax.fori_loop(0, devices, turn, start)


def doc_index(positions, bounds):
    return jnp.sum((positions[:, None] >= bounds[None, :]).astype(jnp.int32), axis=1)


def combine_states(earlier, later):
    return (earlier[0] * later[0], later[0] * earlier[1] + later[1])


def block_shards(projections, attention_order, doc_lengths, short_filter, decay_rate, residue, skip_gain):
    block_total = lax.axis_size("ctx")
    block_index = lax.axis_index("ctx")
    channels = short_filter.shape[2]
    row_count = projections.shape[1] * lax.axis_size("ch")
    slot_rows = row_count // block_total
    modes = decay_rate.shape[1]
    groups = decay_rate.shape[0]
    group_width = channels // groups
    first_row = block_index * row_count
    routing = attention_order.reshape(block_total, block_total, slot_rows)
    arrived = lax.dynamic_slice_in_dim(routing, block_index, 1, 1).reshape(row_count) - first_row
    placer = (arrived[None, :] == jnp.arange(row_count, dtype=jnp.int32)[:, None]).astype(
        jnp.bfloat16
    )
    received = lax.all_to_all(
        lax.all_to_all(projections, "ch", split_axis=2, concat_axis=1, tiled=True),
        "ctx",
        split_axis=1,
        concat_axis=1,
        tiled=True,
    )
    ordered = jnp.einsum(
        "tr,prc->ptc", placer, received, preferred_element_type=jnp.float32
    ).astype(jnp.bfloat16)
    earlier_rows = from_behind(ordered[:, row_count - 2 :, :], "ctx", 1)
    bounds = jnp.sum(jnp.tril(jnp.broadcast_to(doc_lengths, (doc_lengths.size,) * 2)), axis=1)
    span_docs = doc_index(first_row - 2 + jnp.arange(row_count + 2, dtype=jnp.int32), bounds)
    current = span_docs[2:]
    previous_doc = span_docs[1]
    widened = jnp.concatenate([earlier_rows, ordered], axis=1)
    featured = jnp.zeros((3, row_count, channels), jnp.float32)
    for offset in range(3):
        same_doc = (span_docs[2 - offset : 2 - offset + row_count] == current).astype(jnp.float32)
        featured = (
            featured
            + short_filter[:, offset, None, :]
            * widened[:, 2 - offset : 2 - offset + row_count, :]
            * same_doc[None, :, None]
        )
    gated = lax.optimization_barrier((featured[1] * featured[2]).astype(jnp.bfloat16))
    coefficient = residue * jnp.sqrt(1.0 - jnp.exp(-2.0 * decay_rate))
    steps_float = jnp.arange(row_count, dtype=jnp.float32)
    tokens_index = jnp.arange(row_count, dtype=jnp.int32)
    causal = (
        (tokens_index[:, None] >= tokens_index[None, :]) & (current[:, None] == current[None, :])
    ).astype(jnp.float32)
    end_same = (current == current[row_count - 1]).astype(jnp.float32)
    carry_same = (current == previous_doc).astype(jnp.float32)
    group_batch = 8
    batch_count = groups // group_batch
    rate_blocks = decay_rate.reshape(batch_count, group_batch, modes)
    coeff_blocks = coefficient.reshape(batch_count, group_batch, modes)
    gated_blocks = jnp.moveaxis(
        gated.reshape(row_count, batch_count, group_batch * group_width), 1, 0
    )

    def local_block(inputs):
        rate_rows, coeffs, values = inputs
        values_wide = values.astype(jnp.float32).reshape(row_count, group_batch, group_width)
        falling = coeffs[:, :, None] * jnp.exp(-rate_rows[:, :, None] * steps_float[None, None, :])
        rising = jnp.exp(rate_rows[:, :, None] * steps_float[None, None, :])
        toeplitz = jnp.einsum("bmt,bms->bts", falling, rising, precision=highest) * causal[None]
        filtered_part = jnp.einsum("bts,sbc->tbc", toeplitz, values_wide, precision=highest)
        ending = (
            jnp.exp(-rate_rows[:, :, None] * (row_count - 1.0 - steps_float)[None, None, :])
            * end_same[None, None, :]
        )
        state_part = jnp.einsum("bms,sbc->mbc", ending, values_wide, precision=highest)
        return (
            filtered_part.reshape(row_count, group_batch * group_width),
            state_part.reshape(modes, group_batch * group_width),
        )

    filtered_blocks, state_blocks = lax.map(local_block, (rate_blocks, coeff_blocks, gated_blocks))
    filtered = jnp.moveaxis(filtered_blocks, 0, 1).reshape(row_count, channels)
    state_end = jnp.moveaxis(state_blocks, 0, 1).reshape(modes, channels)
    rate_wide = jnp.repeat(decay_rate.T, group_width, axis=1)
    linking = (previous_doc == current[row_count - 1]).astype(jnp.float32)
    factor = jnp.exp(-rate_wide * row_count) * linking
    carried = entering(
        (factor, state_end),
        "ctx",
        combine_states,
        (jnp.ones_like(factor), jnp.zeros_like(state_end)),
    )[1]
    reaching = coefficient[:, :, None] * jnp.exp(
        -decay_rate[:, :, None] * (steps_float + 1.0)[None, None, :]
    )
    incoming = jnp.einsum(
        "gmt,mgc->tgc", reaching, carried.reshape(modes, groups, group_width), precision=highest
    ).reshape(row_count, channels)
    combined = (
        filtered + incoming * carry_same[:, None] + skip_gain[None, :] * gated.astype(jnp.float32)
    )
    mixed = (featured[0] * combined).astype(jnp.bfloat16)
    returned = jnp.einsum("tr,tc->rc", placer, mixed, preferred_element_type=jnp.float32).astype(
        jnp.bfloat16
    )
    return lax.all_to_all(
        lax.all_to_all(returned, "ctx", split_axis=0, concat_axis=0, tiled=True),
        "ch",
        split_axis=0,
        concat_axis=1,
        tiled=True,
    )


def doc_of(positions, bounds):
    found = jnp.zeros(positions.shape, jnp.int32) if positions.shape else jnp.int32(0)
    for bound in bounds:
        found = found + (positions >= bound).astype(jnp.int32)
    return found


def channel_kernel(
    sizes,
    projections,
    order,
    lengths,
    short_filter,
    skip_gain,
    rates,
    coefficients,
    rate_rows,
    out,
    held,
    back,
    placers,
    returners,
    toeplitz,
    endings,
    reaching,
    gate,
    query,
    sources,
    filtered,
    doc_masks,
    end_mask,
    carry_mask,
    local_sems,
    there_send,
    there_recv,
    home_send,
    home_recv,
):
    blocks, shares, length, slot, fold, chunks, filters, modes = sizes
    devices = blocks * shares
    rows = length // shares
    slots = rows // slot
    per_chunk = LANES // fold
    width = chunks * LANES
    docs = lengths.shape[0]
    channels = short_filter.shape[2]
    ctx = lax.axis_index("ctx")
    here = ctx * shares + lax.axis_index("ch")
    own_columns = ctx * width

    def place(device):
        return {"ctx": device // shares, "ch": device % shares}

    def first_column(device, chunk):
        first = (device % shares) * channels + (device // shares) * width + chunk * LANES
        return pl.multiple_of(first, LANES)

    def there(chunk, target, source):
        return pltpu.make_async_remote_copy(
            src_ref=projections.at[:, :, pl.ds(first_column(target, chunk), LANES)],
            dst_ref=held.at[chunk, source],
            send_sem=there_send.at[chunk, target],
            recv_sem=there_recv.at[chunk, source],
            device_id=place(target),
            device_id_type=pl.DeviceIdType.MESH,
        )

    def home(chunk, target, source):
        return pltpu.make_async_remote_copy(
            src_ref=back.at[chunk, target],
            dst_ref=out.at[:, pl.ds(first_column(source, chunk), LANES)],
            send_sem=home_send.at[chunk, target],
            recv_sem=home_recv.at[chunk, source],
            device_id=place(target),
            device_id_type=pl.DeviceIdType.MESH,
        )

    def local_there(chunk):
        return pltpu.make_async_copy(
            projections.at[:, :, pl.ds(first_column(here, chunk), LANES)],
            held.at[chunk, here],
            local_sems.at[0, chunk],
        )

    def local_home(chunk):
        return pltpu.make_async_copy(
            back.at[chunk, here],
            out.at[:, pl.ds(first_column(here, chunk), LANES)],
            local_sems.at[1, chunk],
        )

    def others(act):
        def turn(step, carry):
            act((here + step) % devices)
            return carry

        lax.fori_loop(1, devices, turn, 0)

    barrier = pltpu.get_barrier_semaphore()
    others(
        lambda device: pl.semaphore_signal(
            barrier, inc=1, device_id=place(device), device_id_type=pl.DeviceIdType.MESH
        )
    )
    pl.semaphore_wait(barrier, devices - 1)
    for chunk in range(chunks):
        others(lambda device: there(chunk, device, here).start())
        local_there(chunk).start()

    bounds = []
    total = jnp.int32(0)
    for index in range(docs):
        total = total + lengths[index]
        bounds.append(total)

    square = (length, length)
    down = lax.broadcasted_iota(jnp.int32, square, 0)
    across = lax.broadcasted_iota(jnp.int32, square, 1)

    def make_placers(block, carry):
        placer = (order[block] == down).astype(jnp.float32)
        placers[block] = placer.astype(jnp.bfloat16)
        returners[block] = placer.T.astype(jnp.bfloat16)
        return carry

    lax.fori_loop(0, blocks, make_placers, 0)

    steps = lax.broadcasted_iota(jnp.int32, (modes, length), 1).astype(jnp.float32)

    def split(value):
        high = value.astype(jnp.bfloat16)
        low = (value - high.astype(jnp.float32)).astype(jnp.bfloat16)
        return high, low

    def make_filters(index, carry):
        rate = rates[index]
        falling = coefficients[index] * jnp.exp(-rate * steps)
        impulse = jnp.sum(falling, axis=0, keepdims=True)
        turned = pltpu.roll(
            jnp.broadcast_to(impulse, square), 0, axis=1, stride=1, stride_axis=0
        )
        toeplitz[index] = jnp.where(across >= down, turned, 0.0).astype(jnp.bfloat16)
        high, low = split(jnp.exp(-rate * (length - 1.0 - steps)))
        endings[index, 0] = jnp.concatenate([high, high, high], axis=0)
        endings[index, 1] = jnp.concatenate([low, low, low], axis=0)
        high, low = split(coefficients[index] * jnp.exp(-rate * (steps + 1.0)))
        reaching[index] = jnp.concatenate([high, high, low], axis=0)
        return carry

    lax.fori_loop(0, filters, make_filters, 0)

    strip = (blocks * fold, length)
    strip_block = lax.broadcasted_iota(jnp.int32, strip, 0) // fold
    strip_doc = doc_of(strip_block * length + lax.broadcasted_iota(jnp.int32, strip, 1), bounds)
    for doc in range(docs):
        doc_masks[doc] = (strip_doc == doc).astype(jnp.float32)
    last_doc = doc_of(strip_block * length + (length - 1), bounds)
    end_mask[...] = (strip_doc == last_doc).astype(jnp.bfloat16)
    first_doc = doc_of(strip_block * length - 1, bounds)
    carry_mask[...] = (strip_doc == first_doc).astype(jnp.float32)

    tile = (length, LANES)
    tile_rows = lax.broadcasted_iota(jnp.int32, tile, 0)
    lane = lax.broadcasted_iota(jnp.int32, (blocks * fold, 3 * modes), 1)
    middle = (lane >= modes) & (lane < 2 * modes)

    def fresh(positions):
        found = positions == 0
        for bound in bounds[:-1]:
            found = found | (positions == bound)
        return found

    def work(chunk):
        columns = pl.ds(pl.multiple_of(own_columns + chunk * LANES, LANES), LANES)
        taps = [[short_filter[j, tap : tap + 1, columns] for tap in range(3)] for j in range(3)]
        skip = skip_gain[:, columns]
        grouped = held.at[chunk]

        def gather(block, tails):
            share, inner = block // slots, block % slots
            at = pl.ds(pl.multiple_of(inner * slot, slot), slot)
            positions = block * length + tile_rows
            keep_one = jnp.where(fresh(positions), 0.0, 1.0)
            keep_two = jnp.where(fresh(positions - 1), 0.0, keep_one)
            placer = placers[block]
            featured, new_tails = [], []
            for j in range(3):
                arrived = jnp.concatenate(
                    [grouped[a * shares + share, j, at, :] for a in range(blocks)], axis=0
                )
                ordered = jnp.dot(placer, arrived, preferred_element_type=jnp.float32)
                longer = jnp.concatenate([tails[j], ordered], axis=0)
                featured.append(
                    taps[j][0] * ordered
                    + taps[j][1] * longer[7 : 7 + length] * keep_one
                    + taps[j][2] * longer[6 : 6 + length] * keep_two
                )
                new_tails.append(ordered[length - 8 :])
            product = (featured[1] * featured[2]).astype(jnp.bfloat16)
            query[block] = featured[0]
            gate[block] = product
            turned = product.astype(jnp.float32).T.astype(jnp.bfloat16)
            to = pl.ds(pl.multiple_of(block * fold, fold), fold)
            for group in range(per_chunk):
                sources[group, to, :] = turned[group * fold : (group + 1) * fold]
            return tuple(new_tails)

        lax.fori_loop(
            0, blocks, gather, tuple(jnp.zeros((8, LANES), jnp.float32) for _ in range(3))
        )

        def convolve(group, carry):
            index = chunk * per_chunk + group
            values = sources[group]
            kernel_rows = toeplitz[index]
            ended = values * end_mask[...]
            contract = (((1,), (1,)), ((), ()))
            states = lax.dot_general(
                ended, endings[index, 0], contract, preferred_element_type=jnp.float32
            ) + lax.dot_general(
                ended, endings[index, 1], contract, preferred_element_type=jnp.float32
            )
            factor = jnp.exp(-rate_rows[index] * float(length))
            state = jnp.zeros((fold, 3 * modes), jnp.float32)
            entering_states = []
            for block in range(blocks):
                entering_states.append(state)
                before = doc_of(jnp.int32(block * length - 1), bounds)
                after = doc_of(jnp.int32(block * length + length - 1), bounds)
                linked = (before == after).astype(jnp.float32)
                state = factor * linked * state + states[block * fold : (block + 1) * fold]
            entered = jnp.concatenate(entering_states, axis=0)
            high = entered.astype(jnp.bfloat16).astype(jnp.float32)
            parts = jnp.where(middle, entered - high, high).astype(jnp.bfloat16)
            total = carry_mask[...] * jnp.dot(
                parts, reaching[index], preferred_element_type=jnp.float32
            )
            for doc in range(docs):
                mask = doc_masks[doc]
                total = total + mask * jnp.dot(
                    values * mask.astype(jnp.bfloat16),
                    kernel_rows,
                    preferred_element_type=jnp.float32,
                )
            at = pl.ds(pl.multiple_of(group * fold, fold), fold)
            for block in range(blocks):
                filtered[block, at, :] = total[block * fold : (block + 1) * fold]
            return carry

        lax.fori_loop(0, per_chunk, convolve, 0)

        def mix(block, carry):
            share, inner = block // slots, block % slots
            at = pl.ds(pl.multiple_of(inner * slot, slot), slot)
            combined = filtered[block].T + skip * gate[block].astype(jnp.float32)
            mixed = (query[block] * combined).astype(jnp.bfloat16)
            returned = jnp.dot(
                returners[block], mixed, preferred_element_type=jnp.float32
            ).astype(jnp.bfloat16)
            for a in range(blocks):
                back[chunk, a * shares + share, at, :] = returned[a * slot : (a + 1) * slot]
            return carry

        lax.fori_loop(0, blocks, mix, 0)

    for chunk in range(chunks):
        others(lambda device: there(chunk, here, device).wait_recv())
        local_there(chunk).wait()
        work(chunk)
        others(lambda device: home(chunk, device, here).start())
        local_home(chunk).start()
    for chunk in range(chunks):
        others(lambda device: there(chunk, device, here).wait_send())
        others(lambda device: home(chunk, device, here).wait_send())
        others(lambda device: home(chunk, here, device).wait_recv())
        local_home(chunk).wait()


def channel_shards(
    projections, attention_order, doc_lengths, short_filter, decay_rate, residue, skip_gain
):
    blocks, shares = lax.axis_size("ctx"), lax.axis_size("ch")
    devices = blocks * shares
    rows, model = projections.shape[1:]
    length = rows * shares
    slot = length // blocks
    channels = short_filter.shape[2]
    groups, modes = decay_rate.shape
    fold = channels // groups
    width = model // devices
    chunks = width // LANES
    filters = width // fold
    docs = doc_lengths.shape[0]
    coefficient = residue * jnp.sqrt(1.0 - jnp.exp(-2.0 * decay_rate))
    first = lax.axis_index("ctx") * filters
    rates = lax.dynamic_slice_in_dim(decay_rate, first, filters, 0)
    coefficients = lax.dynamic_slice_in_dim(coefficient, first, filters, 0)
    order = attention_order.reshape(blocks, blocks, slot).transpose(1, 0, 2)
    order = order.reshape(blocks, 1, length)
    order = order - (jnp.arange(blocks, dtype=jnp.int32) * length)[:, None, None]
    sizes = (blocks, shares, length, slot, fold, chunks, filters, modes)
    vmem = pl.BlockSpec(memory_space=pltpu.VMEM)
    strip = (blocks * fold, length)
    per_chunk = LANES // fold
    return pl.pallas_call(
        functools.partial(channel_kernel, sizes),
        out_shape=jax.ShapeDtypeStruct((rows, model), jnp.bfloat16),
        in_specs=[
            pl.BlockSpec(memory_space=pl.ANY),
            vmem,
            pl.BlockSpec(memory_space=pltpu.SMEM),
            vmem,
            vmem,
            vmem,
            vmem,
            vmem,
        ],
        out_specs=pl.BlockSpec(memory_space=pl.ANY),
        scratch_shapes=[
            pltpu.VMEM((chunks, devices, 3, rows, LANES), jnp.bfloat16),
            pltpu.VMEM((chunks, devices, rows, LANES), jnp.bfloat16),
            pltpu.VMEM((blocks, length, length), jnp.bfloat16),
            pltpu.VMEM((blocks, length, length), jnp.bfloat16),
            pltpu.VMEM((filters, length, length), jnp.bfloat16),
            pltpu.VMEM((filters, 2, 3 * modes, length), jnp.bfloat16),
            pltpu.VMEM((filters, 3 * modes, length), jnp.bfloat16),
            pltpu.VMEM((blocks, length, LANES), jnp.bfloat16),
            pltpu.VMEM((blocks, length, LANES), jnp.float32),
            pltpu.VMEM((per_chunk,) + strip, jnp.bfloat16),
            pltpu.VMEM((blocks, LANES, length), jnp.float32),
            pltpu.VMEM((docs,) + strip, jnp.float32),
            pltpu.VMEM(strip, jnp.bfloat16),
            pltpu.VMEM(strip, jnp.float32),
            pltpu.SemaphoreType.DMA((2, chunks)),
            pltpu.SemaphoreType.DMA((chunks, devices)),
            pltpu.SemaphoreType.DMA((chunks, devices)),
            pltpu.SemaphoreType.DMA((chunks, devices)),
            pltpu.SemaphoreType.DMA((chunks, devices)),
        ],
        compiler_params=pltpu.CompilerParams(
            collective_id=0, has_side_effects=True, vmem_limit_bytes=48 * 1024 * 1024
        ),
    )(
        projections,
        order,
        doc_lengths,
        short_filter,
        skip_gain[None, :],
        rates[:, :, None],
        coefficients[:, :, None],
        jnp.tile(rates, (1, 3))[:, None, :],
    )


def shards(projections, attention_order, doc_lengths, short_filter, decay_rate, residue, skip_gain):
    devices = lax.axis_size("ctx") * lax.axis_size("ch")
    slot = projections.shape[1] * lax.axis_size("ch") // lax.axis_size("ctx")
    whole_tiles = projections.shape[2] % (devices * LANES) == 0 and slot % 16 == 0
    run = channel_shards if whole_tiles else block_shards
    return run(
        projections, attention_order, doc_lengths, short_filter, decay_rate, residue, skip_gain
    )


def solution(mesh):
    placed = (
        P(None, ("ctx", "ch"), None),
        P(),
        P(),
        P(None, None, "ch"),
        P("ch", None),
        P("ch", None),
        P("ch"),
    )
    return jax.shard_map(
        shards, mesh=mesh, in_specs=placed, out_specs=P(("ctx", "ch"), None), check_vma=False
    )
```

```python
import functools
import math

import jax
import jax.numpy as jnp
from jax import lax
from jax.experimental import pallas as pl
from jax.experimental.pallas import tpu as pltpu
from jax.sharding import PartitionSpec as P

LANES = 128

highest = lax.Precision.HIGHEST


def from_behind(value, axis, steps):
    count = lax.axis_size(axis)
    first, last = (max(0, -steps), min(count, count - steps))
    return lax.ppermute(value, axis, [(source, source + steps) for source in range(first, last)])


def entering(value, axis, combine, identity):
    devices, here = (lax.axis_size(axis), lax.axis_index(axis))
    everything = jax.tree.map(lambda part: lax.all_gather(part, axis), value)
    start = jax.tree.map(
        lambda part, zero: jnp.broadcast_to(jnp.asarray(zero, part.dtype), part.shape),
        value,
        identity,
    )

    def turn(k, before):
        reached = k < here
        new = combine(before, jax.tree.map(lambda part: part[k], everything))
        return jax.tree.map(lambda a, b: jnp.where(reached, a, b), new, before)

    return lax.fori_loop(0, devices, turn, start)


def doc_index(positions, bounds):
    return jnp.sum((positions[:, None] >= bounds[None, :]).astype(jnp.int32), axis=1)


def combine_states(earlier, later):
    return (earlier[0] * later[0], later[0] * earlier[1] + later[1])


def block_shards(projections, attention_order, doc_lengths, short_filter, decay_rate, residue, skip_gain):
    block_total = lax.axis_size("ctx")
    block_index = lax.axis_index("ctx")
    channels = short_filter.shape[2]
    row_count = projections.shape[1] * lax.axis_size("ch")
    slot_rows = row_count // block_total
    modes = decay_rate.shape[1]
    groups = decay_rate.shape[0]
    group_width = channels // groups
    first_row = block_index * row_count
    routing = attention_order.reshape(block_total, block_total, slot_rows)
    arrived = lax.dynamic_slice_in_dim(routing, block_index, 1, 1).reshape(row_count) - first_row
    placer = (arrived[None, :] == jnp.arange(row_count, dtype=jnp.int32)[:, None]).astype(
        jnp.bfloat16
    )
    received = lax.all_to_all(
        lax.all_to_all(projections, "ch", split_axis=2, concat_axis=1, tiled=True),
        "ctx",
        split_axis=1,
        concat_axis=1,
        tiled=True,
    )
    ordered = jnp.einsum(
        "tr,prc->ptc", placer, received, preferred_element_type=jnp.float32
    ).astype(jnp.bfloat16)
    earlier_rows = from_behind(ordered[:, row_count - 2 :, :], "ctx", 1)
    bounds = jnp.sum(jnp.tril(jnp.broadcast_to(doc_lengths, (doc_lengths.size,) * 2)), axis=1)
    span_docs = doc_index(first_row - 2 + jnp.arange(row_count + 2, dtype=jnp.int32), bounds)
    current = span_docs[2:]
    previous_doc = span_docs[1]
    widened = jnp.concatenate([earlier_rows, ordered], axis=1)
    featured = jnp.zeros((3, row_count, channels), jnp.float32)
    for offset in range(3):
        same_doc = (span_docs[2 - offset : 2 - offset + row_count] == current).astype(jnp.float32)
        featured = (
            featured
            + short_filter[:, offset, None, :]
            * widened[:, 2 - offset : 2 - offset + row_count, :]
            * same_doc[None, :, None]
        )
    gated = lax.optimization_barrier((featured[1] * featured[2]).astype(jnp.bfloat16))
    coefficient = residue * jnp.sqrt(1.0 - jnp.exp(-2.0 * decay_rate))
    steps_float = jnp.arange(row_count, dtype=jnp.float32)
    tokens_index = jnp.arange(row_count, dtype=jnp.int32)
    causal = (
        (tokens_index[:, None] >= tokens_index[None, :]) & (current[:, None] == current[None, :])
    ).astype(jnp.float32)
    end_same = (current == current[row_count - 1]).astype(jnp.float32)
    carry_same = (current == previous_doc).astype(jnp.float32)
    group_batch = 8
    batch_count = groups // group_batch
    rate_blocks = decay_rate.reshape(batch_count, group_batch, modes)
    coeff_blocks = coefficient.reshape(batch_count, group_batch, modes)
    gated_blocks = jnp.moveaxis(
        gated.reshape(row_count, batch_count, group_batch * group_width), 1, 0
    )

    def local_block(inputs):
        rate_rows, coeffs, values = inputs
        values_wide = values.astype(jnp.float32).reshape(row_count, group_batch, group_width)
        falling = coeffs[:, :, None] * jnp.exp(-rate_rows[:, :, None] * steps_float[None, None, :])
        rising = jnp.exp(rate_rows[:, :, None] * steps_float[None, None, :])
        toeplitz = jnp.einsum("bmt,bms->bts", falling, rising, precision=highest) * causal[None]
        filtered_part = jnp.einsum("bts,sbc->tbc", toeplitz, values_wide, precision=highest)
        ending = (
            jnp.exp(-rate_rows[:, :, None] * (row_count - 1.0 - steps_float)[None, None, :])
            * end_same[None, None, :]
        )
        state_part = jnp.einsum("bms,sbc->mbc", ending, values_wide, precision=highest)
        return (
            filtered_part.reshape(row_count, group_batch * group_width),
            state_part.reshape(modes, group_batch * group_width),
        )

    filtered_blocks, state_blocks = lax.map(local_block, (rate_blocks, coeff_blocks, gated_blocks))
    filtered = jnp.moveaxis(filtered_blocks, 0, 1).reshape(row_count, channels)
    state_end = jnp.moveaxis(state_blocks, 0, 1).reshape(modes, channels)
    rate_wide = jnp.repeat(decay_rate.T, group_width, axis=1)
    linking = (previous_doc == current[row_count - 1]).astype(jnp.float32)
    factor = jnp.exp(-rate_wide * row_count) * linking
    carried = entering(
        (factor, state_end),
        "ctx",
        combine_states,
        (jnp.ones_like(factor), jnp.zeros_like(state_end)),
    )[1]
    reaching = coefficient[:, :, None] * jnp.exp(
        -decay_rate[:, :, None] * (steps_float + 1.0)[None, None, :]
    )
    incoming = jnp.einsum(
        "gmt,mgc->tgc", reaching, carried.reshape(modes, groups, group_width), precision=highest
    ).reshape(row_count, channels)
    combined = (
        filtered + incoming * carry_same[:, None] + skip_gain[None, :] * gated.astype(jnp.float32)
    )
    mixed = (featured[0] * combined).astype(jnp.bfloat16)
    returned = jnp.einsum("tr,tc->rc", placer, mixed, preferred_element_type=jnp.float32).astype(
        jnp.bfloat16
    )
    return lax.all_to_all(
        lax.all_to_all(returned, "ctx", split_axis=0, concat_axis=0, tiled=True),
        "ch",
        split_axis=0,
        concat_axis=1,
        tiled=True,
    )


def doc_of(positions, bounds):
    found = jnp.zeros(positions.shape, jnp.int32) if positions.shape else jnp.int32(0)
    for bound in bounds:
        found = found + (positions >= bound).astype(jnp.int32)
    return found


def channel_kernel(
    sizes,
    projections,
    order,
    lengths,
    short_filter,
    skip_gain,
    rates,
    coefficients,
    rate_rows,
    out,
    held,
    back,
    placers,
    returners,
    toeplitz,
    endings,
    reaching,
    gate,
    query,
    sources,
    filtered,
    doc_masks,
    end_mask,
    carry_mask,
    local_sems,
    there_send,
    there_recv,
    home_send,
    home_recv,
):
    blocks, shares, length, slot, fold, chunks, filters, modes = sizes
    devices = blocks * shares
    rows = length // shares
    slots = rows // slot
    per_chunk = LANES // fold
    width = chunks * LANES
    docs = lengths.shape[0]
    channels = short_filter.shape[2]
    ctx = lax.axis_index("ctx")
    here = ctx * shares + lax.axis_index("ch")
    own_columns = ctx * width

    def place(device):
        return {"ctx": device // shares, "ch": device % shares}

    def first_column(device, chunk):
        first = (device % shares) * channels + (device // shares) * width + chunk * LANES
        return pl.multiple_of(first, LANES)

    def there(chunk, target, source):
        return pltpu.make_async_remote_copy(
            src_ref=projections.at[:, :, pl.ds(first_column(target, chunk), LANES)],
            dst_ref=held.at[chunk, source],
            send_sem=there_send.at[chunk, target],
            recv_sem=there_recv.at[chunk, source],
            device_id=place(target),
            device_id_type=pl.DeviceIdType.MESH,
        )

    def home(chunk, target, source):
        return pltpu.make_async_remote_copy(
            src_ref=back.at[chunk, target],
            dst_ref=out.at[:, pl.ds(first_column(source, chunk), LANES)],
            send_sem=home_send.at[chunk, target],
            recv_sem=home_recv.at[chunk, source],
            device_id=place(target),
            device_id_type=pl.DeviceIdType.MESH,
        )

    def local_there(chunk):
        return pltpu.make_async_copy(
            projections.at[:, :, pl.ds(first_column(here, chunk), LANES)],
            held.at[chunk, here],
            local_sems.at[0, chunk],
        )

    def local_home(chunk):
        return pltpu.make_async_copy(
            back.at[chunk, here],
            out.at[:, pl.ds(first_column(here, chunk), LANES)],
            local_sems.at[1, chunk],
        )

    stride = devices // 2 - 3 if math.gcd(devices // 2 - 3, devices) == 1 else 1

    def others(act):
        def turn(step, carry):
            act((here + step * stride) % devices)
            return carry

        lax.fori_loop(1, devices, turn, 0)

    barrier = pltpu.get_barrier_semaphore()
    others(
        lambda device: pl.semaphore_signal(
            barrier, inc=1, device_id=place(device), device_id_type=pl.DeviceIdType.MESH
        )
    )
    pl.semaphore_wait(barrier, devices - 1)
    for chunk in range(chunks):
        others(lambda device: there(chunk, device, here).start())
        local_there(chunk).start()

    bounds = []
    total = jnp.int32(0)
    for index in range(docs):
        total = total + lengths[index]
        bounds.append(total)

    square = (length, length)
    down = lax.broadcasted_iota(jnp.int32, square, 0)
    across = lax.broadcasted_iota(jnp.int32, square, 1)

    def make_placers(block, carry):
        placer = (order[block] == down).astype(jnp.float32)
        placers[block] = placer.astype(jnp.bfloat16)
        returners[block] = placer.T.astype(jnp.bfloat16)
        return carry

    lax.fori_loop(0, blocks, make_placers, 0)

    steps = lax.broadcasted_iota(jnp.int32, (modes, length), 1).astype(jnp.float32)

    def split(value):
        high = value.astype(jnp.bfloat16)
        low = (value - high.astype(jnp.float32)).astype(jnp.bfloat16)
        return high, low

    def make_filters(index, carry):
        rate = rates[index]
        falling = coefficients[index] * jnp.exp(-rate * steps)
        impulse = jnp.sum(falling, axis=0, keepdims=True)
        turned = pltpu.roll(
            jnp.broadcast_to(impulse, square), 0, axis=1, stride=1, stride_axis=0
        )
        toeplitz[index] = jnp.where(across >= down, turned, 0.0).astype(jnp.bfloat16)
        high, low = split(jnp.exp(-rate * (length - 1.0 - steps)))
        endings[index, 0] = jnp.concatenate([high, high, high], axis=0)
        endings[index, 1] = jnp.concatenate([low, low, low], axis=0)
        high, low = split(coefficients[index] * jnp.exp(-rate * (steps + 1.0)))
        reaching[index] = jnp.concatenate([high, high, low], axis=0)
        return carry

    lax.fori_loop(0, filters, make_filters, 0)

    strip = (blocks * fold, length)
    strip_block = lax.broadcasted_iota(jnp.int32, strip, 0) // fold
    strip_doc = doc_of(strip_block * length + lax.broadcasted_iota(jnp.int32, strip, 1), bounds)
    for doc in range(docs):
        doc_masks[doc] = (strip_doc == doc).astype(jnp.float32)
    last_doc = doc_of(strip_block * length + (length - 1), bounds)
    end_mask[...] = (strip_doc == last_doc).astype(jnp.bfloat16)
    first_doc = doc_of(strip_block * length - 1, bounds)
    carry_mask[...] = (strip_doc == first_doc).astype(jnp.float32)

    tile = (length, LANES)
    tile_rows = lax.broadcasted_iota(jnp.int32, tile, 0)
    lane = lax.broadcasted_iota(jnp.int32, (blocks * fold, 3 * modes), 1)
    middle = (lane >= modes) & (lane < 2 * modes)

    def fresh(positions):
        found = positions == 0
        for bound in bounds[:-1]:
            found = found | (positions == bound)
        return found

    def work(chunk):
        columns = pl.ds(pl.multiple_of(own_columns + chunk * LANES, LANES), LANES)
        taps = [[short_filter[j, tap : tap + 1, columns] for tap in range(3)] for j in range(3)]
        skip = skip_gain[:, columns]
        grouped = held.at[chunk]

        def gather(block, tails):
            share, inner = block // slots, block % slots
            at = pl.ds(pl.multiple_of(inner * slot, slot), slot)
            positions = block * length + tile_rows
            keep_one = jnp.where(fresh(positions), 0.0, 1.0)
            keep_two = jnp.where(fresh(positions - 1), 0.0, keep_one)
            placer = placers[block]
            featured, new_tails = [], []
            for j in range(3):
                arrived = jnp.concatenate(
                    [grouped[a * shares + share, j, at, :] for a in range(blocks)], axis=0
                )
                ordered = jnp.dot(placer, arrived, preferred_element_type=jnp.float32)
                longer = jnp.concatenate([tails[j], ordered], axis=0)
                featured.append(
                    taps[j][0] * ordered
                    + taps[j][1] * longer[7 : 7 + length] * keep_one
                    + taps[j][2] * longer[6 : 6 + length] * keep_two
                )
                new_tails.append(ordered[length - 8 :])
            product = (featured[1] * featured[2]).astype(jnp.bfloat16)
            query[block] = featured[0]
            gate[block] = product
            turned = product.astype(jnp.float32).T.astype(jnp.bfloat16)
            to = pl.ds(pl.multiple_of(block * fold, fold), fold)
            for group in range(per_chunk):
                sources[group, to, :] = turned[group * fold : (group + 1) * fold]
            return tuple(new_tails)

        lax.fori_loop(
            0, blocks, gather, tuple(jnp.zeros((8, LANES), jnp.float32) for _ in range(3))
        )

        def convolve(group, carry):
            index = chunk * per_chunk + group
            values = sources[group]
            kernel_rows = toeplitz[index]
            ended = values * end_mask[...]
            contract = (((1,), (1,)), ((), ()))
            states = lax.dot_general(
                ended, endings[index, 0], contract, preferred_element_type=jnp.float32
            ) + lax.dot_general(
                ended, endings[index, 1], contract, preferred_element_type=jnp.float32
            )
            factor = jnp.exp(-rate_rows[index] * float(length))
            state = jnp.zeros((fold, 3 * modes), jnp.float32)
            entering_states = []
            for block in range(blocks):
                entering_states.append(state)
                before = doc_of(jnp.int32(block * length - 1), bounds)
                after = doc_of(jnp.int32(block * length + length - 1), bounds)
                linked = (before == after).astype(jnp.float32)
                state = factor * linked * state + states[block * fold : (block + 1) * fold]
            entered = jnp.concatenate(entering_states, axis=0)
            high = entered.astype(jnp.bfloat16).astype(jnp.float32)
            parts = jnp.where(middle, entered - high, high).astype(jnp.bfloat16)
            total = carry_mask[...] * jnp.dot(
                parts, reaching[index], preferred_element_type=jnp.float32
            )
            for doc in range(docs):
                mask = doc_masks[doc]
                total = total + mask * jnp.dot(
                    values * mask.astype(jnp.bfloat16),
                    kernel_rows,
                    preferred_element_type=jnp.float32,
                )
            at = pl.ds(pl.multiple_of(group * fold, fold), fold)
            for block in range(blocks):
                filtered[block, at, :] = total[block * fold : (block + 1) * fold]
            return carry

        lax.fori_loop(0, per_chunk, convolve, 0)

        def mix(block, carry):
            share, inner = block // slots, block % slots
            at = pl.ds(pl.multiple_of(inner * slot, slot), slot)
            combined = filtered[block].T + skip * gate[block].astype(jnp.float32)
            mixed = (query[block] * combined).astype(jnp.bfloat16)
            returned = jnp.dot(
                returners[block], mixed, preferred_element_type=jnp.float32
            ).astype(jnp.bfloat16)
            for a in range(blocks):
                back[chunk, a * shares + share, at, :] = returned[a * slot : (a + 1) * slot]
            return carry

        lax.fori_loop(0, blocks, mix, 0)

    for chunk in range(chunks):
        others(lambda device: there(chunk, here, device).wait_recv())
        local_there(chunk).wait()
        work(chunk)
        others(lambda device: home(chunk, device, here).start())
        local_home(chunk).start()
    for chunk in range(chunks):
        others(lambda device: there(chunk, device, here).wait_send())
        others(lambda device: home(chunk, device, here).wait_send())
        others(lambda device: home(chunk, here, device).wait_recv())
        local_home(chunk).wait()


def channel_shards(
    projections, attention_order, doc_lengths, short_filter, decay_rate, residue, skip_gain
):
    blocks, shares = lax.axis_size("ctx"), lax.axis_size("ch")
    devices = blocks * shares
    rows, model = projections.shape[1:]
    length = rows * shares
    slot = length // blocks
    channels = short_filter.shape[2]
    groups, modes = decay_rate.shape
    fold = channels // groups
    width = model // devices
    chunks = width // LANES
    filters = width // fold
    docs = doc_lengths.shape[0]
    coefficient = residue * jnp.sqrt(1.0 - jnp.exp(-2.0 * decay_rate))
    first = lax.axis_index("ctx") * filters
    rates = lax.dynamic_slice_in_dim(decay_rate, first, filters, 0)
    coefficients = lax.dynamic_slice_in_dim(coefficient, first, filters, 0)
    order = attention_order.reshape(blocks, blocks, slot).transpose(1, 0, 2)
    order = order.reshape(blocks, 1, length)
    order = order - (jnp.arange(blocks, dtype=jnp.int32) * length)[:, None, None]
    sizes = (blocks, shares, length, slot, fold, chunks, filters, modes)
    vmem = pl.BlockSpec(memory_space=pltpu.VMEM)
    strip = (blocks * fold, length)
    per_chunk = LANES // fold
    return pl.pallas_call(
        functools.partial(channel_kernel, sizes),
        out_shape=jax.ShapeDtypeStruct((rows, model), jnp.bfloat16),
        in_specs=[
            pl.BlockSpec(memory_space=pl.ANY),
            vmem,
            pl.BlockSpec(memory_space=pltpu.SMEM),
            vmem,
            vmem,
            vmem,
            vmem,
            vmem,
        ],
        out_specs=pl.BlockSpec(memory_space=pl.ANY),
        scratch_shapes=[
            pltpu.VMEM((chunks, devices, 3, rows, LANES), jnp.bfloat16),
            pltpu.VMEM((chunks, devices, rows, LANES), jnp.bfloat16),
            pltpu.VMEM((blocks, length, length), jnp.bfloat16),
            pltpu.VMEM((blocks, length, length), jnp.bfloat16),
            pltpu.VMEM((filters, length, length), jnp.bfloat16),
            pltpu.VMEM((filters, 2, 3 * modes, length), jnp.bfloat16),
            pltpu.VMEM((filters, 3 * modes, length), jnp.bfloat16),
            pltpu.VMEM((blocks, length, LANES), jnp.bfloat16),
            pltpu.VMEM((blocks, length, LANES), jnp.float32),
            pltpu.VMEM((per_chunk,) + strip, jnp.bfloat16),
            pltpu.VMEM((blocks, LANES, length), jnp.float32),
            pltpu.VMEM((docs,) + strip, jnp.float32),
            pltpu.VMEM(strip, jnp.bfloat16),
            pltpu.VMEM(strip, jnp.float32),
            pltpu.SemaphoreType.DMA((2, chunks)),
            pltpu.SemaphoreType.DMA((chunks, devices)),
            pltpu.SemaphoreType.DMA((chunks, devices)),
            pltpu.SemaphoreType.DMA((chunks, devices)),
            pltpu.SemaphoreType.DMA((chunks, devices)),
        ],
        compiler_params=pltpu.CompilerParams(
            collective_id=0, has_side_effects=True, vmem_limit_bytes=48 * 1024 * 1024
        ),
    )(
        projections,
        order,
        doc_lengths,
        short_filter,
        skip_gain[None, :],
        rates[:, :, None],
        coefficients[:, :, None],
        jnp.tile(rates, (1, 3))[:, None, :],
    )


def shards(projections, attention_order, doc_lengths, short_filter, decay_rate, residue, skip_gain):
    devices = lax.axis_size("ctx") * lax.axis_size("ch")
    slot = projections.shape[1] * lax.axis_size("ch") // lax.axis_size("ctx")
    whole_tiles = projections.shape[2] % (devices * LANES) == 0 and slot % 16 == 0
    run = channel_shards if whole_tiles else block_shards
    return run(
        projections, attention_order, doc_lengths, short_filter, decay_rate, residue, skip_gain
    )


def solution(mesh):
    placed = (
        P(None, ("ctx", "ch"), None),
        P(),
        P(),
        P(None, None, "ch"),
        P("ch", None),
        P("ch", None),
        P("ch"),
    )
    return jax.shard_map(
        shards, mesh=mesh, in_specs=placed, out_specs=P(("ctx", "ch"), None), check_vma=False
    )
```

```python
import functools
import math

import jax
import jax.numpy as jnp
from jax import lax
from jax.experimental import pallas as pl
from jax.experimental.pallas import tpu as pltpu
from jax.sharding import PartitionSpec as P

LANES = 128

highest = lax.Precision.HIGHEST


def from_behind(value, axis, steps):
    count = lax.axis_size(axis)
    first, last = (max(0, -steps), min(count, count - steps))
    return lax.ppermute(value, axis, [(source, source + steps) for source in range(first, last)])


def entering(value, axis, combine, identity):
    devices, here = (lax.axis_size(axis), lax.axis_index(axis))
    everything = jax.tree.map(lambda part: lax.all_gather(part, axis), value)
    start = jax.tree.map(
        lambda part, zero: jnp.broadcast_to(jnp.asarray(zero, part.dtype), part.shape),
        value,
        identity,
    )

    def turn(k, before):
        reached = k < here
        new = combine(before, jax.tree.map(lambda part: part[k], everything))
        return jax.tree.map(lambda a, b: jnp.where(reached, a, b), new, before)

    return lax.fori_loop(0, devices, turn, start)


def doc_index(positions, bounds):
    return jnp.sum((positions[:, None] >= bounds[None, :]).astype(jnp.int32), axis=1)


def combine_states(earlier, later):
    return (earlier[0] * later[0], later[0] * earlier[1] + later[1])


def block_shards(projections, attention_order, doc_lengths, short_filter, decay_rate, residue, skip_gain):
    block_total = lax.axis_size("ctx")
    block_index = lax.axis_index("ctx")
    channels = short_filter.shape[2]
    row_count = projections.shape[1] * lax.axis_size("ch")
    slot_rows = row_count // block_total
    modes = decay_rate.shape[1]
    groups = decay_rate.shape[0]
    group_width = channels // groups
    first_row = block_index * row_count
    routing = attention_order.reshape(block_total, block_total, slot_rows)
    arrived = lax.dynamic_slice_in_dim(routing, block_index, 1, 1).reshape(row_count) - first_row
    placer = (arrived[None, :] == jnp.arange(row_count, dtype=jnp.int32)[:, None]).astype(
        jnp.bfloat16
    )
    received = lax.all_to_all(
        lax.all_to_all(projections, "ch", split_axis=2, concat_axis=1, tiled=True),
        "ctx",
        split_axis=1,
        concat_axis=1,
        tiled=True,
    )
    ordered = jnp.einsum(
        "tr,prc->ptc", placer, received, preferred_element_type=jnp.float32
    ).astype(jnp.bfloat16)
    earlier_rows = from_behind(ordered[:, row_count - 2 :, :], "ctx", 1)
    bounds = jnp.sum(jnp.tril(jnp.broadcast_to(doc_lengths, (doc_lengths.size,) * 2)), axis=1)
    span_docs = doc_index(first_row - 2 + jnp.arange(row_count + 2, dtype=jnp.int32), bounds)
    current = span_docs[2:]
    previous_doc = span_docs[1]
    widened = jnp.concatenate([earlier_rows, ordered], axis=1)
    featured = jnp.zeros((3, row_count, channels), jnp.float32)
    for offset in range(3):
        same_doc = (span_docs[2 - offset : 2 - offset + row_count] == current).astype(jnp.float32)
        featured = (
            featured
            + short_filter[:, offset, None, :]
            * widened[:, 2 - offset : 2 - offset + row_count, :]
            * same_doc[None, :, None]
        )
    gated = lax.optimization_barrier((featured[1] * featured[2]).astype(jnp.bfloat16))
    coefficient = residue * jnp.sqrt(1.0 - jnp.exp(-2.0 * decay_rate))
    steps_float = jnp.arange(row_count, dtype=jnp.float32)
    tokens_index = jnp.arange(row_count, dtype=jnp.int32)
    causal = (
        (tokens_index[:, None] >= tokens_index[None, :]) & (current[:, None] == current[None, :])
    ).astype(jnp.float32)
    end_same = (current == current[row_count - 1]).astype(jnp.float32)
    carry_same = (current == previous_doc).astype(jnp.float32)
    group_batch = 8
    batch_count = groups // group_batch
    rate_blocks = decay_rate.reshape(batch_count, group_batch, modes)
    coeff_blocks = coefficient.reshape(batch_count, group_batch, modes)
    gated_blocks = jnp.moveaxis(
        gated.reshape(row_count, batch_count, group_batch * group_width), 1, 0
    )

    def local_block(inputs):
        rate_rows, coeffs, values = inputs
        values_wide = values.astype(jnp.float32).reshape(row_count, group_batch, group_width)
        falling = coeffs[:, :, None] * jnp.exp(-rate_rows[:, :, None] * steps_float[None, None, :])
        rising = jnp.exp(rate_rows[:, :, None] * steps_float[None, None, :])
        toeplitz = jnp.einsum("bmt,bms->bts", falling, rising, precision=highest) * causal[None]
        filtered_part = jnp.einsum("bts,sbc->tbc", toeplitz, values_wide, precision=highest)
        ending = (
            jnp.exp(-rate_rows[:, :, None] * (row_count - 1.0 - steps_float)[None, None, :])
            * end_same[None, None, :]
        )
        state_part = jnp.einsum("bms,sbc->mbc", ending, values_wide, precision=highest)
        return (
            filtered_part.reshape(row_count, group_batch * group_width),
            state_part.reshape(modes, group_batch * group_width),
        )

    filtered_blocks, state_blocks = lax.map(local_block, (rate_blocks, coeff_blocks, gated_blocks))
    filtered = jnp.moveaxis(filtered_blocks, 0, 1).reshape(row_count, channels)
    state_end = jnp.moveaxis(state_blocks, 0, 1).reshape(modes, channels)
    rate_wide = jnp.repeat(decay_rate.T, group_width, axis=1)
    linking = (previous_doc == current[row_count - 1]).astype(jnp.float32)
    factor = jnp.exp(-rate_wide * row_count) * linking
    carried = entering(
        (factor, state_end),
        "ctx",
        combine_states,
        (jnp.ones_like(factor), jnp.zeros_like(state_end)),
    )[1]
    reaching = coefficient[:, :, None] * jnp.exp(
        -decay_rate[:, :, None] * (steps_float + 1.0)[None, None, :]
    )
    incoming = jnp.einsum(
        "gmt,mgc->tgc", reaching, carried.reshape(modes, groups, group_width), precision=highest
    ).reshape(row_count, channels)
    combined = (
        filtered + incoming * carry_same[:, None] + skip_gain[None, :] * gated.astype(jnp.float32)
    )
    mixed = (featured[0] * combined).astype(jnp.bfloat16)
    returned = jnp.einsum("tr,tc->rc", placer, mixed, preferred_element_type=jnp.float32).astype(
        jnp.bfloat16
    )
    return lax.all_to_all(
        lax.all_to_all(returned, "ctx", split_axis=0, concat_axis=0, tiled=True),
        "ch",
        split_axis=0,
        concat_axis=1,
        tiled=True,
    )


def doc_of(positions, bounds):
    found = jnp.zeros(positions.shape, jnp.int32) if positions.shape else jnp.int32(0)
    for bound in bounds:
        found = found + (positions >= bound).astype(jnp.int32)
    return found


def channel_kernel(
    sizes,
    projections,
    order,
    lengths,
    short_filter,
    skip_gain,
    rates,
    coefficients,
    rate_rows,
    out,
    held,
    back,
    placers,
    returners,
    toeplitz,
    endings,
    reaching,
    gate,
    query,
    sources,
    filtered,
    doc_masks,
    end_mask,
    carry_mask,
    local_sems,
    there_send,
    there_recv,
    home_send,
    home_recv,
):
    blocks, shares, length, slot, fold, chunks, filters, modes = sizes
    devices = blocks * shares
    rows = length // shares
    slots = rows // slot
    per_chunk = LANES // fold
    width = chunks * LANES
    docs = lengths.shape[0]
    channels = short_filter.shape[2]
    ctx = lax.axis_index("ctx")
    here = ctx * shares + lax.axis_index("ch")
    own_columns = ctx * width

    def place(device):
        return {"ctx": device // shares, "ch": device % shares}

    def first_column(device, chunk):
        first = (device % shares) * channels + (device // shares) * width + chunk * LANES
        return pl.multiple_of(first, LANES)

    def there(chunk, target, source):
        return pltpu.make_async_remote_copy(
            src_ref=projections.at[:, :, pl.ds(first_column(target, chunk), LANES)],
            dst_ref=held.at[chunk, source],
            send_sem=there_send.at[chunk, target],
            recv_sem=there_recv.at[chunk, source],
            device_id=place(target),
            device_id_type=pl.DeviceIdType.MESH,
        )

    def home(chunk, target, source):
        return pltpu.make_async_remote_copy(
            src_ref=back.at[chunk, target],
            dst_ref=out.at[:, pl.ds(first_column(source, chunk), LANES)],
            send_sem=home_send.at[chunk, target],
            recv_sem=home_recv.at[chunk, source],
            device_id=place(target),
            device_id_type=pl.DeviceIdType.MESH,
        )

    def local_there(chunk):
        return pltpu.make_async_copy(
            projections.at[:, :, pl.ds(first_column(here, chunk), LANES)],
            held.at[chunk, here],
            local_sems.at[0, chunk],
        )

    def local_home(chunk):
        return pltpu.make_async_copy(
            back.at[chunk, here],
            out.at[:, pl.ds(first_column(here, chunk), LANES)],
            local_sems.at[1, chunk],
        )

    stride = devices // 2 - 3 if math.gcd(devices // 2 - 3, devices) == 1 else 1

    def others(act):
        def turn(step, carry):
            act((here + step * stride) % devices)
            return carry

        lax.fori_loop(1, devices, turn, 0)

    barrier = pltpu.get_barrier_semaphore()
    others(
        lambda device: pl.semaphore_signal(
            barrier, inc=1, device_id=place(device), device_id_type=pl.DeviceIdType.MESH
        )
    )
    pl.semaphore_wait(barrier, devices - 1)
    for chunk in range(chunks):
        others(lambda device: there(chunk, device, here).start())
        local_there(chunk).start()

    bounds = []
    total = jnp.int32(0)
    for index in range(docs):
        total = total + lengths[index]
        bounds.append(total)

    square = (length, length)
    down = lax.broadcasted_iota(jnp.int32, square, 0)
    across = lax.broadcasted_iota(jnp.int32, square, 1)

    def make_placers(block, carry):
        placer = (order[block] == down).astype(jnp.float32)
        placers[block] = placer.astype(jnp.bfloat16)
        returners[block] = placer.T.astype(jnp.bfloat16)
        return carry

    lax.fori_loop(0, blocks, make_placers, 0)

    steps = lax.broadcasted_iota(jnp.int32, (modes, length), 1).astype(jnp.float32)

    def split(value):
        high = value.astype(jnp.bfloat16)
        low = (value - high.astype(jnp.float32)).astype(jnp.bfloat16)
        return high, low

    def make_filters(index, carry):
        rate = rates[index]
        falling = coefficients[index] * jnp.exp(-rate * steps)
        impulse = jnp.sum(falling, axis=0, keepdims=True)
        turned = pltpu.roll(
            jnp.broadcast_to(impulse, square), 0, axis=1, stride=1, stride_axis=0
        )
        toeplitz[index] = jnp.where(across >= down, turned, 0.0).astype(jnp.bfloat16)
        high, low = split(jnp.exp(-rate * (length - 1.0 - steps)))
        endings[index, 0] = jnp.concatenate([high, high, high], axis=0)
        endings[index, 1] = jnp.concatenate([low, low, low], axis=0)
        high, low = split(coefficients[index] * jnp.exp(-rate * (steps + 1.0)))
        reaching[index] = jnp.concatenate([high, high, low], axis=0)
        return carry

    lax.fori_loop(0, filters, make_filters, 0)

    strip = (blocks * fold, length)
    strip_block = lax.broadcasted_iota(jnp.int32, strip, 0) // fold
    strip_doc = doc_of(strip_block * length + lax.broadcasted_iota(jnp.int32, strip, 1), bounds)
    for doc in range(docs):
        doc_masks[doc] = (strip_doc == doc).astype(jnp.float32)
    last_doc = doc_of(strip_block * length + (length - 1), bounds)
    end_mask[...] = (strip_doc == last_doc).astype(jnp.bfloat16)
    first_doc = doc_of(strip_block * length - 1, bounds)
    carry_mask[...] = (strip_doc == first_doc).astype(jnp.float32)

    tile = (length, LANES)
    tile_rows = lax.broadcasted_iota(jnp.int32, tile, 0)
    lane = lax.broadcasted_iota(jnp.int32, (blocks * fold, 3 * modes), 1)
    middle = (lane >= modes) & (lane < 2 * modes)

    def fresh(positions):
        found = positions == 0
        for bound in bounds[:-1]:
            found = found | (positions == bound)
        return found

    def work(chunk):
        columns = pl.ds(pl.multiple_of(own_columns + chunk * LANES, LANES), LANES)
        taps = [[short_filter[j, tap : tap + 1, columns] for tap in range(3)] for j in range(3)]
        skip = skip_gain[:, columns]
        grouped = held.at[chunk]

        def gather(block, tails):
            share, inner = block // slots, block % slots
            at = pl.ds(pl.multiple_of(inner * slot, slot), slot)
            positions = block * length + tile_rows
            keep_one = jnp.where(fresh(positions), 0.0, 1.0)
            keep_two = jnp.where(fresh(positions - 1), 0.0, keep_one)
            placer = placers[block]
            featured, new_tails = [], []
            for j in range(3):
                arrived = jnp.concatenate(
                    [grouped[a * shares + share, j, at, :] for a in range(blocks)], axis=0
                )
                ordered = jnp.dot(placer, arrived, preferred_element_type=jnp.float32)
                longer = jnp.concatenate([tails[j], ordered], axis=0)
                featured.append(
                    taps[j][0] * ordered
                    + taps[j][1] * longer[7 : 7 + length] * keep_one
                    + taps[j][2] * longer[6 : 6 + length] * keep_two
                )
                new_tails.append(ordered[length - 8 :])
            product = (featured[1] * featured[2]).astype(jnp.bfloat16)
            query[block] = featured[0]
            gate[block] = product
            turned = product.astype(jnp.float32).T.astype(jnp.bfloat16)
            to = pl.ds(pl.multiple_of(block * fold, fold), fold)
            for group in range(per_chunk):
                sources[group, to, :] = turned[group * fold : (group + 1) * fold]
            return tuple(new_tails)

        lax.fori_loop(
            0,
            blocks,
            gather,
            tuple(jnp.zeros((8, LANES), jnp.float32) for _ in range(3)),
            unroll=2,
        )

        def convolve(group, carry):
            index = chunk * per_chunk + group
            values = sources[group]
            kernel_rows = toeplitz[index]
            ended = values * end_mask[...]
            contract = (((1,), (1,)), ((), ()))
            states = lax.dot_general(
                ended, endings[index, 0], contract, preferred_element_type=jnp.float32
            ) + lax.dot_general(
                ended, endings[index, 1], contract, preferred_element_type=jnp.float32
            )
            factor = jnp.exp(-rate_rows[index] * float(length))
            state = jnp.zeros((fold, 3 * modes), jnp.float32)
            entering_states = []
            for block in range(blocks):
                entering_states.append(state)
                before = doc_of(jnp.int32(block * length - 1), bounds)
                after = doc_of(jnp.int32(block * length + length - 1), bounds)
                linked = (before == after).astype(jnp.float32)
                state = factor * linked * state + states[block * fold : (block + 1) * fold]
            entered = jnp.concatenate(entering_states, axis=0)
            high = entered.astype(jnp.bfloat16).astype(jnp.float32)
            parts = jnp.where(middle, entered - high, high).astype(jnp.bfloat16)
            total = carry_mask[...] * jnp.dot(
                parts, reaching[index], preferred_element_type=jnp.float32
            )
            for doc in range(docs):
                mask = doc_masks[doc]
                total = total + mask * jnp.dot(
                    values * mask.astype(jnp.bfloat16),
                    kernel_rows,
                    preferred_element_type=jnp.float32,
                )
            at = pl.ds(pl.multiple_of(group * fold, fold), fold)
            for block in range(blocks):
                filtered[block, at, :] = total[block * fold : (block + 1) * fold]
            return carry

        lax.fori_loop(0, per_chunk, convolve, 0, unroll=2)

        def mix(block, carry):
            share, inner = block // slots, block % slots
            at = pl.ds(pl.multiple_of(inner * slot, slot), slot)
            combined = filtered[block].T + skip * gate[block].astype(jnp.float32)
            mixed = (query[block] * combined).astype(jnp.bfloat16)
            returned = jnp.dot(
                returners[block], mixed, preferred_element_type=jnp.float32
            ).astype(jnp.bfloat16)
            for a in range(blocks):
                back[chunk, a * shares + share, at, :] = returned[a * slot : (a + 1) * slot]
            return carry

        lax.fori_loop(0, blocks, mix, 0, unroll=2)

    for chunk in range(chunks):
        others(lambda device: there(chunk, here, device).wait_recv())
        local_there(chunk).wait()
        work(chunk)
        others(lambda device: home(chunk, device, here).start())
        local_home(chunk).start()
    for chunk in range(chunks):
        others(lambda device: there(chunk, device, here).wait_send())
        others(lambda device: home(chunk, device, here).wait_send())
        others(lambda device: home(chunk, here, device).wait_recv())
        local_home(chunk).wait()


def channel_shards(
    projections, attention_order, doc_lengths, short_filter, decay_rate, residue, skip_gain
):
    blocks, shares = lax.axis_size("ctx"), lax.axis_size("ch")
    devices = blocks * shares
    rows, model = projections.shape[1:]
    length = rows * shares
    slot = length // blocks
    channels = short_filter.shape[2]
    groups, modes = decay_rate.shape
    fold = channels // groups
    width = model // devices
    chunks = width // LANES
    filters = width // fold
    docs = doc_lengths.shape[0]
    coefficient = residue * jnp.sqrt(1.0 - jnp.exp(-2.0 * decay_rate))
    first = lax.axis_index("ctx") * filters
    rates = lax.dynamic_slice_in_dim(decay_rate, first, filters, 0)
    coefficients = lax.dynamic_slice_in_dim(coefficient, first, filters, 0)
    order = attention_order.reshape(blocks, blocks, slot).transpose(1, 0, 2)
    order = order.reshape(blocks, 1, length)
    order = order - (jnp.arange(blocks, dtype=jnp.int32) * length)[:, None, None]
    sizes = (blocks, shares, length, slot, fold, chunks, filters, modes)
    vmem = pl.BlockSpec(memory_space=pltpu.VMEM)
    strip = (blocks * fold, length)
    per_chunk = LANES // fold
    return pl.pallas_call(
        functools.partial(channel_kernel, sizes),
        out_shape=jax.ShapeDtypeStruct((rows, model), jnp.bfloat16),
        in_specs=[
            pl.BlockSpec(memory_space=pl.ANY),
            vmem,
            pl.BlockSpec(memory_space=pltpu.SMEM),
            vmem,
            vmem,
            vmem,
            vmem,
            vmem,
        ],
        out_specs=pl.BlockSpec(memory_space=pl.ANY),
        scratch_shapes=[
            pltpu.VMEM((chunks, devices, 3, rows, LANES), jnp.bfloat16),
            pltpu.VMEM((chunks, devices, rows, LANES), jnp.bfloat16),
            pltpu.VMEM((blocks, length, length), jnp.bfloat16),
            pltpu.VMEM((blocks, length, length), jnp.bfloat16),
            pltpu.VMEM((filters, length, length), jnp.bfloat16),
            pltpu.VMEM((filters, 2, 3 * modes, length), jnp.bfloat16),
            pltpu.VMEM((filters, 3 * modes, length), jnp.bfloat16),
            pltpu.VMEM((blocks, length, LANES), jnp.bfloat16),
            pltpu.VMEM((blocks, length, LANES), jnp.float32),
            pltpu.VMEM((per_chunk,) + strip, jnp.bfloat16),
            pltpu.VMEM((blocks, LANES, length), jnp.float32),
            pltpu.VMEM((docs,) + strip, jnp.float32),
            pltpu.VMEM(strip, jnp.bfloat16),
            pltpu.VMEM(strip, jnp.float32),
            pltpu.SemaphoreType.DMA((2, chunks)),
            pltpu.SemaphoreType.DMA((chunks, devices)),
            pltpu.SemaphoreType.DMA((chunks, devices)),
            pltpu.SemaphoreType.DMA((chunks, devices)),
            pltpu.SemaphoreType.DMA((chunks, devices)),
        ],
        compiler_params=pltpu.CompilerParams(
            collective_id=0, has_side_effects=True, vmem_limit_bytes=48 * 1024 * 1024
        ),
    )(
        projections,
        order,
        doc_lengths,
        short_filter,
        skip_gain[None, :],
        rates[:, :, None],
        coefficients[:, :, None],
        jnp.tile(rates, (1, 3))[:, None, :],
    )


def shards(projections, attention_order, doc_lengths, short_filter, decay_rate, residue, skip_gain):
    devices = lax.axis_size("ctx") * lax.axis_size("ch")
    slot = projections.shape[1] * lax.axis_size("ch") // lax.axis_size("ctx")
    whole_tiles = projections.shape[2] % (devices * LANES) == 0 and slot % 16 == 0
    run = channel_shards if whole_tiles else block_shards
    return run(
        projections, attention_order, doc_lengths, short_filter, decay_rate, residue, skip_gain
    )


def solution(mesh):
    placed = (
        P(None, ("ctx", "ch"), None),
        P(),
        P(),
        P(None, None, "ch"),
        P("ch", None),
        P("ch", None),
        P("ch"),
    )
    return jax.shard_map(
        shards, mesh=mesh, in_specs=placed, out_specs=P(("ctx", "ch"), None), check_vma=False
    )
```
